256 devices in a mesh: own: 64 (over x, z, core), col: 4 (over y).
Axes of the slice: x: 4, y: 4, z: 8, core: 2. Of those that a mesh axis runs over, the one named last changes fastest.
Arguments:
- anc_store: float32 [128, 512, 512], P('own', None, 'col'), may hold values from -6 to 6
- block_map: int32 [128], replicated, may hold values from 0 to 127, as said below
- anc_refs: int32 [128, 3, 3], replicated, may hold values from 0 to 127, as said below
- factor1: bfloat16 [128, 3, 512, 512], P('own', None, 'col'), may hold values from -0.15625 to 0.15625
- dinv1: float32 [128, 512, 512], P('own', 'col'), may hold values from -6 to 6
- factor2: bfloat16 [128, 3, 512, 512], P('own', None, 'col'), may hold values from -0.15625 to 0.15625
- dinv2: float32 [128, 512, 512], P('own', 'col'), may hold values from -6 to 6
- parent: int32 [128], P('own'), may hold values from 0 to 1
- picked: int32 [128, 2], P('own'), may hold values from 0 to 2, as said below
Outputs:
- cross1: float32 [128, 3, 512, 512], P('own', None, 'col')
- diag1: float32 [128, 512, 512], P('own', 'col')
- cross2: float32 [128, 3, 512, 512], P('own', None, 'col')
- diag2: float32 [128, 512, 512], P('own', 'col')
The draws below stay inside these ranges and needn't reach their ends.
Inputs may be any that keep to these rules, and one draw needn't show every extreme that they name: A permutation: tile t is held by owner block_map[t] // 2 in its slot block_map[t] % 2. `anc_refs`: the 18 references of one owner's level-1 blocks name tiles held by any single owner at most 1 times, and exactly 1 times for some owner. `picked`: entries of one row are distinct.
All inputs are finite; a program needn't handle non-finite values.
Results may differ from the reference program's by a relative error of at most 0.0036.
Values may be sent and summed in bfloat16 or wider, within the bound.
A program may use at most 64 MiB of HBM per device.

```python
import jax
import jax.numpy as jnp
from jax import lax

B = 512
A = 3
SN1 = 2
TA_DEV = 2
BLOCKS = 128
TILES = 128


def store_layout(key):
    owner_total = TILES // TA_DEV
    positions = jax.random.permutation(jax.random.fold_in(key, 11), TILES).astype(jnp.int32)
    holder = jnp.argsort(positions).astype(jnp.int32)
    request_total = SN1 * A * A
    scores = jax.random.randint(jax.random.fold_in(key, 12), (owner_total, owner_total), 0, 1 << 16) * owner_total + jnp.arange(owner_total)[None, :]
    ranking = jnp.argsort(scores, axis=1)
    owner_of = ranking[:, jnp.arange(request_total) % owner_total]
    slot_of = jax.random.randint(jax.random.fold_in(key, 13), (owner_total, request_total), 0, TA_DEV)
    references = holder[owner_of * TA_DEV + slot_of].reshape(BLOCKS, A, A)
    return (positions, references.astype(jnp.int32))


def draw_block_map(key, part):
    return store_layout(key)[0]


def draw_anc_refs(key, part):
    return store_layout(key)[1]


def draw_picked(key, part):
    scores = jax.random.randint(jax.random.fold_in(key, 21), (BLOCKS, A), 0, 1 << 16) * A + jnp.arange(A)[None, :]
    ranking = jnp.argsort(scores, axis=1)
    return ranking[:, :A - 1].astype(jnp.int32)


def set_ends(array, rng, least, high):
    index_at = [jax.random.randint(jax.random.fold_in(rng, axis), (), 0, length) for axis, length in enumerate(array.shape)]
    main_axis = array.shape.index(max(array.shape))
    beside = index_at[:main_axis] + [(index_at[main_axis] + 1) % array.shape[main_axis]] + index_at[main_axis + 1:]
    return array.at[tuple(index_at)].set(least).at[tuple(beside)].set(high)


def block_scale(rng, extent, pieces, smallest, largest):
    def one(dim, parts):
        heights = jax.random.uniform(jax.random.fold_in(jax.random.fold_in(rng, 6), dim), (parts,), jnp.float32, smallest / len(pieces), largest / len(pieces))
        return jnp.repeat(jnp.exp(heights), extent[dim] // parts).reshape((-1,) + (1,) * (len(extent) - dim - 1))

    gain = one(*pieces[0])
    for cut in pieces[1:]:
        gain = gain * one(*cut)
    return gain


def noise(key, shape, width, most, shards=(), kind=jnp.bfloat16):
    result = width * jax.random.normal(key, shape, jnp.float32)
    if shards:
        result = result * block_scale(key, shape, shards, -0.22, 0.18)
    return jnp.clip(result, -most, most).astype(kind)


def setup_inputs(seed: int = 0) -> dict:
    splits = jax.random.split(jax.random.key(seed), 10)
    return {
        "anc_store": noise(splits[0], (TILES, B, B), 1.0, 6.0, ((0, 64), (2, 4)), jnp.float32),
        "block_map": draw_block_map(jax.random.fold_in(splits[9], 71), 0),
        "anc_refs": draw_anc_refs(jax.random.fold_in(splits[9], 71), 0),
        "factor1": noise(splits[3], (BLOCKS, A, B, B), (A * B) ** -0.5, 0.15625, ((0, 64), (2, 4))),
        "dinv1": noise(splits[4], (BLOCKS, B, B), 1.0, 6.0, ((0, 64), (1, 4)), jnp.float32),
        "factor2": noise(splits[5], (BLOCKS, A, B, B), (A * B) ** -0.5, 0.15625, ((0, 64), (2, 4))),
        "dinv2": noise(splits[6], (BLOCKS, B, B), 1.0, 6.0, ((0, 64), (1, 4)), jnp.float32),
        "parent": set_ends(jax.random.randint(splits[7], (BLOCKS,), 0, SN1), jax.random.fold_in(splits[7], 1), 0, SN1 - 1).astype(jnp.int32),
        "picked": draw_picked(jax.random.fold_in(splits[9], 71), 0),
    }


def one_block(sigma, factor, dinv):
    sigma32 = sigma.astype(jnp.float32)
    factor32 = factor.astype(jnp.float32)
    cross = -jnp.einsum('ikrs,ksj->irj', sigma32, factor32, precision=lax.Precision.HIGHEST)
    cross_low = cross.astype(jnp.bfloat16)
    diag_block = dinv - jnp.einsum('ksj,ksl->jl', factor32, cross_low.astype(jnp.float32), precision=lax.Precision.HIGHEST)
    return cross, diag_block


def reference(anc_store, block_map, anc_refs, factor1, dinv1, factor2, dinv2, parent, picked):
    anc_copy = anc_store.astype(jnp.bfloat16)

    def ancestor_tiles(refs):
        return anc_copy[block_map[refs]]

    def level_one(block_id):
        return one_block(ancestor_tiles(anc_refs[block_id]), factor1[block_id], dinv1[block_id])

    cross1, diag1 = lax.map(level_one, jnp.arange(BLOCKS, dtype=jnp.int32))
    cross_low1 = cross1.astype(jnp.bfloat16)
    diag_low1 = diag1.astype(jnp.bfloat16)

    def level_two(block_id):
        parent_id = block_id - block_id % SN1 + parent[block_id]
        choose = picked[block_id]
        parent_rows = cross_low1[parent_id]
        parent_tiles = ancestor_tiles(anc_refs[parent_id])
        top_row = jnp.concatenate([diag_low1[parent_id].T[None], jnp.swapaxes(parent_rows[choose], 1, 2)], 0)
        inner_tiles = parent_tiles[choose][:, choose]
        lower_rows = jnp.concatenate([parent_rows[choose][:, None], inner_tiles], 1)
        sigma = jnp.concatenate([top_row[None], lower_rows], 0)
        return one_block(sigma, factor2[block_id], dinv2[block_id])

    cross2, diag2 = lax.map(level_two, jnp.arange(BLOCKS, dtype=jnp.int32))
    return cross1, diag1, cross2, diag2
```

```python
import jax
import jax.numpy as jnp
from jax import lax
from jax.sharding import PartitionSpec as P


def assemble(low, cols, diag_cols, tiles, choose):
    top = jnp.concatenate([diag_cols.T[None], jnp.swapaxes(cols[choose], 1, 2)], 0)
    lower = jnp.concatenate([low[choose][:, None], tiles[choose][:, choose]], 1)
    return jnp.concatenate([top[None], lower], 0)


def solve_cross(tiles, factor):
    return -jnp.einsum("mikrs,mksj->mirj", tiles, factor, preferred_element_type=jnp.float32)


def correction(factor, cols):
    return jnp.einsum("mksj,mksl->mjl", factor, cols, preferred_element_type=jnp.float32)


def to_columns(rows):
    last = rows.ndim - 1
    return lax.all_to_all(rows, "col", split_axis=last, concat_axis=last - 1, tiled=True)


def to_rows(columns):
    last = columns.ndim - 1
    return lax.all_to_all(columns, "col", split_axis=last - 1, concat_axis=last, tiled=True)


def per_device(anc_store, block_map, anc_refs, factor1, dinv1, factor2, dinv2, parent, picked):
    blocks_here = factor1.shape[0]
    me = lax.axis_index("own")
    rows = to_rows(anc_store.astype(jnp.bfloat16))
    store = lax.all_gather(rows, "own", axis=0, tiled=True)
    whole1 = lax.all_gather(factor1, "col", axis=2, tiled=True)
    whole2 = lax.all_gather(factor2, "col", axis=2, tiled=True)
    dinv_cols1 = to_columns(dinv1)
    refs = lax.dynamic_slice_in_dim(anc_refs, me * blocks_here, blocks_here, 0)
    tiles1 = store[block_map[refs]]
    cross1 = solve_cross(tiles1, whole1)
    low1 = cross1.astype(jnp.bfloat16)
    cols1 = to_columns(low1)
    diag_cols1 = dinv_cols1 - correction(whole1, cols1)
    diag1 = to_rows(diag_cols1)
    tiles2 = jax.vmap(assemble)(
        low1[parent], cols1[parent], diag_cols1.astype(jnp.bfloat16)[parent], tiles1[parent], picked
    )
    cross2 = solve_cross(tiles2, whole2)
    cols2 = to_columns(cross2.astype(jnp.bfloat16))
    diag2 = dinv2 - to_rows(correction(whole2, cols2))
    return (cross1, diag1, cross2, diag2)


def solution(mesh):
    return jax.shard_map(
        per_device,
        mesh=mesh,
        in_specs=(
            P("own", None, "col"),
            P(),
            P(),
            P("own", None, "col", None),
            P("own", "col", None),
            P("own", None, "col", None),
            P("own", "col", None),
            P("own"),
            P("own", None),
        ),
        out_specs=(
            P("own", None, "col", None),
            P("own", "col", None),
            P("own", None, "col", None),
            P("own", "col", None),
        ),
        check_vma=False,
    )
```

```python
import functools

import jax
import jax.numpy as jnp
from jax import lax
from jax.experimental import pallas as pl
from jax.experimental.pallas import tpu as pltpu
from jax.sharding import PartitionSpec as P

X, Z, Y = 4, 8, 4
B, A, W = 512, 3, 128
ROWS_A = 48
F32, BF16 = jnp.float32, jnp.bfloat16


class Wires:
    def __init__(self, send_sems, recv_sems):
        self.send_sems, self.recv_sems = send_sems, recv_sems
        self.names, self.sent = {}, []

    def slot(self, name):
        return self.names.setdefault(name, len(self.names))

    def make(self, name, src, dst, device):
        slot = self.slot(name)
        return pltpu.make_async_remote_copy(
            src_ref=src,
            dst_ref=dst,
            send_sem=self.send_sems.at[slot],
            recv_sem=self.recv_sems.at[slot],
            device_id=device,
            device_id_type=pl.DeviceIdType.MESH,
        )

    def send(self, name, src, dst, device):
        copy = self.make(name, src, dst, device)
        copy.start()
        self.sent.append(copy)

    def wait(self, name, dst, device):
        self.make(name, dst, dst, device).wait_recv()

    def finish(self):
        for copy in self.sent:
            copy.wait_send()


WIRES = 256


def dot(a, b):
    return jnp.dot(a, b, preferred_element_type=F32)


def kernel(
    anc, bmap, refs_all, f1, dinv1, f2, dinv2, parent, picked,
    cross1, diag1, cross2, diag2,
    store, f1w, f2w, anc_v, stage, refs, low, turned, turned2, cols1, cols2, out1, out2,
    part, dcol, dcolt, dlow, dsend1, dsend2, grow, dinv_v, dout,
    send_sems, recv_sems, local_sems,
):
    own, y = lax.axis_index("own"), lax.axis_index("col")
    core = lax.rem(own, 2)
    chip = own // 2
    x, z = chip // Z, lax.rem(chip, Z)

    def at(dx, dz, dcore=0):
        xx, zz = lax.rem(x + dx + X, X), lax.rem(z + dz + Z, Z)
        return (xx * Z + zz) * 2 + (lax.rem(core + dcore, 2) if dcore else core)

    def yat(d):
        return lax.rem(y + d + Y, Y)

    xup, xdn = (at(1, 0), y), (at(-1, 0), y)
    zup, zdn = (at(0, 1), y), (at(0, -1), y)
    mate = (at(0, 0, 1), y)
    ydev = {d: (own, yat(d)) for d in (1, 2, 3)}
    wires = Wires(send_sems, recv_sems)
    held = {}

    def local(name, src, dst):
        slot = held.setdefault(name, len(held))
        return pltpu.make_async_copy(src, dst, local_sems.at[slot])

    def lanes(index):
        return pl.ds(pl.multiple_of(index * W, W), W)

    load_anc = local("anc", anc, anc_v)
    load_anc.start()
    load_refs = local("refs", refs_all.at[pl.ds(own * 2, 2)], refs)
    load_refs.start()
    load_f1 = local("f1", f1, f1w.at[:, :, lanes(y), :])
    load_f1.start()
    load_f2 = local("f2", f2, f2w.at[:, :, lanes(y), :])
    load_f2.start()
    load_dcol = local("dcol", dinv1.at[:, :, lanes(y)], dcol.at[:, lanes(y), :])
    load_dcol.start()
    load_dinv2 = local("dinv2", dinv2, dinv_v)
    load_dinv2.start()

    barrier = pltpu.get_barrier_semaphore()
    peers = [xup, xdn, zup, zdn, mate, ydev[1], ydev[2], ydev[3]]
    for peer in peers:
        pl.semaphore_signal(barrier, inc=1, device_id=peer, device_id_type=pl.DeviceIdType.MESH)
    pl.semaphore_wait(barrier, len(peers))

    load_anc.wait()
    stage[...] = anc_v[...].astype(BF16)
    mine = pl.ds(own * 2, 2)
    for d in (1, 3, 2):
        wires.send(("t", d), stage.at[:, lanes(yat(d)), :], store.at[mine, :, lanes(y)], ydev[d])
    keep = local("t", stage.at[:, lanes(y), :], store.at[mine, :, lanes(y)])
    keep.start()

    def factor_own(tag, src, dst):
        for m, k in ((0, 1), (1, 0)):
            wires.send((tag, "up", m), src.at[m], dst.at[m, :, lanes(y), :], ydev[1])
            wires.send((tag, "dn", k), src.at[k], dst.at[k, :, lanes(y), :], ydev[3])

    def factor_wait(tag, dst, first):
        for way, d, m in (("up", -1, 0 if first else 1), ("dn", 1, 1 if first else 0)):
            piece = dst.at[m, :, lanes(yat(d)), :]
            wires.wait((tag, way, m), piece, ydev[3 if d == -1 else 1])
            if first:
                wires.send((tag, way, "far"), piece, piece, ydev[1 if d == -1 else 3])

    def factor_far(tag, dst):
        wires.wait((tag, "up", "far"), dst.at[0, :, lanes(yat(2)), :], ydev[3])
        wires.wait((tag, "dn", "far"), dst.at[1, :, lanes(yat(2)), :], ydev[1])

    factor_own("f1", f1, f1w)

    keep.wait()
    for d in (1, 3, 2):
        wires.wait(("t", d), store.at[mine, :, lanes(yat(-d))], ydev[4 - d])

    def chunk(path, dx, dz, slot=None, dcore=0):
        tile = at(dx, dz, dcore) * 2
        tiles = pl.ds(tile, 2) if slot is None else pl.ds(tile + slot, 1)
        rows = pl.ds(0, ROWS_A) if path == "a" else pl.ds(ROWS_A, W - ROWS_A)
        return store.at[tiles, rows, :]

    def share(path, dx, dz, slot=None):
        piece = chunk(path, dx, dz, slot)
        wires.send(("mate", path, dx, dz, slot), piece, piece, mate)
        shared.append((path, dx, dz, slot))

    shared = []
    ZWAY = {"up": (zup, zdn, -1), "dn": (zdn, zup, 1)}
    XWAY = {"up": (xup, xdn, -1), "dn": (xdn, xup, 1)}
    SLOT = {"up": 0, "dn": 1}

    def z_send(path, dx, step, slot=None):
        for way, (to, _, sign) in ZWAY.items():
            half = SLOT[way] if step == 4 else slot
            piece = chunk(path, dx, sign * (step - 1), half)
            wires.send(("z", path, dx, way, step), piece, piece, to)

    def x_send(path, dz):
        piece = chunk(path, 0, dz)
        for way, (to, _, _) in XWAY.items():
            wires.send(("x", path, dz, way, 1), piece, piece, to)

    def z_wait(path, dx, step):
        for way, (to, source, sign) in ZWAY.items():
            half = SLOT[way] if step == 4 else None
            piece = chunk(path, dx, sign * step, half)
            wires.wait(("z", path, dx, way, step), piece, source)
            if step < 4:
                half = SLOT[way] if step == 3 else None
                on = chunk(path, dx, sign * step, half)
                wires.send(("z", path, dx, way, step + 1), on, on, to)
                if path == "b":
                    x_send("b", sign * step)
                share(path, dx, sign * step)
        if step == 4:
            if path == "b":
                x_send("b", 4)
            share(path, dx, 4)

    def x_wait(path, dz):
        for way, (to, source, sign) in XWAY.items():
            piece = chunk(path, sign, dz)
            wires.wait(("x", path, dz, way, 1), piece, source)
            on = chunk(path, sign, dz, SLOT[way])
            wires.send(("x", path, dz, way, 2), on, on, to)
            if path == "a":
                z_send("a", sign, 1)
            share(path, sign, dz)

    def x_far(path, dz):
        for way, (_, source, _) in XWAY.items():
            wires.wait(("x", path, dz, way, 2), chunk(path, 2, dz, SLOT[way]), source)
        if path == "a":
            z_send("a", 2, 1)
        share(path, 2, dz)

    x_send("a", 0)
    z_send("b", 0, 1)
    z_send("a", 0, 1)
    x_send("b", 0)
    share("a", 0, 0)
    share("b", 0, 0)

    x_wait("a", 0)
    z_wait("b", 0, 1)
    x_wait("b", 0)
    z_wait("a", 0, 1)
    x_far("a", 0)
    z_wait("b", 0, 2)
    x_far("b", 0)
    factor_wait("f1", f1w, True)
    x_wait("b", -1)
    z_wait("a", -1, 1)
    x_wait("b", 1)
    z_wait("a", 1, 1)
    x_far("b", -1)
    z_wait("b", 0, 3)
    x_far("b", 1)
    factor_wait("f1", f1w, False)
    factor_own("f2", f2, f2w)
    for d in (1, 3, 2):
        wires.send(("d", d), dinv1.at[:, :, lanes(yat(d))], dcol.at[:, lanes(y), :], ydev[d])
    z_wait("a", 2, 1)
    x_wait("b", -2)
    z_wait("a", 0, 2)
    x_wait("b", 2)
    z_wait("b", 0, 4)
    x_far("b", -2)
    x_far("b", 2)
    z_wait("a", -1, 2)
    factor_far("f1", f1w)
    x_wait("b", -3)
    z_wait("a", 1, 2)
    x_wait("b", 3)
    z_wait("a", 2, 2)
    x_far("b", -3)
    x_far("b", 3)
    factor_wait("f2", f2w, True)
    z_wait("a", 0, 3)
    x_wait("b", 4)
    z_wait("a", -1, 3)
    x_far("b", 4)
    z_wait("a", 1, 3)
    z_wait("a", 2, 3)
    for dx in (0, -1, 1, 2):
        z_wait("a", dx, 4)
    for path, dx, dz, slot in shared:
        wires.wait(("mate", path, dx, dz, slot), chunk(path, dx, dz, slot, 1), mate)
    load_refs.wait()
    load_f1.wait()

    def tile(m, i, k):
        return store[bmap[refs[m, i, k]]]

    def stacked(parts):
        return jnp.concatenate(parts, axis=0)

    def give_columns(tag, turned_ref, cols_ref, m):
        for d in (1, 3, 2):
            wires.send(
                (tag, m, d), turned_ref.at[yat(d), m], cols_ref.at[m, :, :, lanes(y)], ydev[d]
            )
        own_part = local((tag, m), turned_ref.at[y, m], cols_ref.at[m, :, :, lanes(y)])
        own_part.start()
        return own_part

    def take_columns(tag, cols_ref, m, own_part):
        own_part.wait()
        for d in (1, 3, 2):
            wires.wait((tag, m, d), cols_ref.at[m, :, :, lanes(yat(-d))], ydev[4 - d])

    def spread(acc, m, n, out_ref, turned_ref, low_ref):
        for i in range(A):
            rows = acc[i * W : (i + 1) * W]
            out_ref[m, i, :, n * 256 : (n + 1) * 256] = rows
            if low_ref is not None:
                low_ref[m, i, :, n * 256 : (n + 1) * 256] = rows.astype(BF16)
            for b in range(2):
                turned_ref[2 * n + b, m, i] = rows[:, b * W : (b + 1) * W].T.astype(BF16)

    kept1, writes = [], []
    for m in range(2):
        for n in range(2):
            acc = 0.0
            for k in range(A):
                acc += dot(
                    stacked([tile(m, i, k) for i in range(A)]), f1w[m, k, :, n * 256 : (n + 1) * 256]
                )
            spread(-acc, m, n, out1, turned, low)
        kept1.append(give_columns("c1", turned, cols1, m))
        write = local(("o1", m), out1.at[m], cross1.at[m])
        write.start()
        writes.append(write)

    factor_wait("f2", f2w, False)
    factor_far("f2", f2w)
    load_f2.wait()
    for m in range(2):
        p = parent[m]
        q = [picked[m, 0], picked[m, 1]]
        for n in range(2):
            acc = 0.0
            for k in range(2):
                acc += dot(
                    stacked([tile(p, q[i], q[k]) for i in range(2)]),
                    f2w[m, k + 1, :, n * 256 : (n + 1) * 256],
                )
            part[m, :, n * 256 : (n + 1) * 256] = acc
    load_dcol.wait()
    for d in (1, 3, 2):
        wires.wait(("d", d), dcol.at[:, lanes(yat(-d)), :], ydev[4 - d])
    for m in range(2):
        for b in range(Y):
            dcolt[m, :, b * W : (b + 1) * W] = dcol[m, b * W : (b + 1) * W, :].T

    def corrections(cols_ref, fw, m):
        return sum(dot(cols_ref[m, k], fw[m, k]) for k in range(A))

    for m in range(2):
        take_columns("c1", cols1, m, kept1[m])
        turned_diag = dcolt[m] - corrections(cols1, f1w, m)
        dlow[m] = turned_diag.astype(BF16)
        for b in range(Y):
            dsend1[b, m] = turned_diag[:, b * W : (b + 1) * W].T

    def give_rows(tag, src, dst):
        for d in (1, 3, 2):
            wires.send((tag, d), src.at[yat(d)], dst.at[:, :, lanes(y)], ydev[d])
        own_part = local(tag, src.at[y], dst.at[:, :, lanes(y)])
        own_part.start()
        return own_part

    def take_rows(tag, dst, own_part):
        own_part.wait()
        for d in (1, 3, 2):
            wires.wait((tag, d), dst.at[:, :, lanes(yat(-d))], ydev[4 - d])

    kept2 = []
    for m in range(2):
        p = parent[m]
        q = [picked[m, 0], picked[m, 1]]
        for n in range(2):
            span = slice(n * 256, (n + 1) * 256)
            acc = dot(stacked([dlow[p], low[p, q[0]], low[p, q[1]]]), f2w[m, 0, :, span])
            top = dot(cols1[p, q[0]], f2w[m, 1, :, span]) + dot(cols1[p, q[1]], f2w[m, 2, :, span])
            acc += stacked([top, part[m, :, span]])
            spread(-acc, m, n, out2, turned2, None)
        kept2.append(give_columns("c2", turned2, cols2, m))
        write = local(("o2", m), out2.at[m], cross2.at[m])
        write.start()
        writes.append(write)
    kept_diag = give_rows("g1", dsend1, diag1)
    load_dinv2.wait()
    for m in range(2):
        take_columns("c2", cols2, m, kept2[m])
        correction = corrections(cols2, f2w, m)
        for b in range(Y):
            dsend2[b, m] = correction[:, b * W : (b + 1) * W].T
    kept_grow = give_rows("g2", dsend2, grow)
    take_rows("g1", diag1, kept_diag)
    take_rows("g2", grow, kept_grow)
    dout[...] = dinv_v[...] - grow[...]
    write = local("o3", dout, diag2)
    write.start()
    writes.append(write)
    for write in writes:
        write.wait()
    wires.finish()


def per_device(anc_store, block_map, anc_refs, factor1, dinv1, factor2, dinv2, parent, picked):
    any_space = pl.BlockSpec(memory_space=pl.ANY)
    smem = pl.BlockSpec(memory_space=pltpu.SMEM)
    flops = 2 * 2 * 2 * (9 + 3) * W * B * B
    return pl.pallas_call(
        kernel,
        out_shape=(
            jax.ShapeDtypeStruct((2, A, W, B), F32),
            jax.ShapeDtypeStruct((2, W, B), F32),
            jax.ShapeDtypeStruct((2, A, W, B), F32),
            jax.ShapeDtypeStruct((2, W, B), F32),
        ),
        in_specs=[any_space, smem, any_space, any_space, any_space, any_space, any_space, smem, smem],
        out_specs=(any_space,) * 4,
        scratch_shapes=[
            pltpu.VMEM((X * Z * 4, W, B), BF16),
            pltpu.VMEM((2, A, B, B), BF16),
            pltpu.VMEM((2, A, B, B), BF16),
            pltpu.VMEM((2, B, W), F32),
            pltpu.VMEM((2, B, W), BF16),
            pltpu.SMEM((2, A, A), jnp.int32),
            pltpu.VMEM((2, A, W, B), BF16),
            pltpu.VMEM((Y, 2, A, W, W), BF16),
            pltpu.VMEM((Y, 2, A, W, W), BF16),
            pltpu.VMEM((2, A, W, B), BF16),
            pltpu.VMEM((2, A, W, B), BF16),
            pltpu.VMEM((2, A, W, B), F32),
            pltpu.VMEM((2, A, W, B), F32),
            pltpu.VMEM((2, 2 * W, B), F32),
            pltpu.VMEM((2, B, W), F32),
            pltpu.VMEM((2, W, B), F32),
            pltpu.VMEM((2, W, B), BF16),
            pltpu.VMEM((Y, 2, W, W), F32),
            pltpu.VMEM((Y, 2, W, W), F32),
            pltpu.VMEM((2, W, B), F32),
            pltpu.VMEM((2, W, B), F32),
            pltpu.VMEM((2, W, B), F32),
            pltpu.SemaphoreType.DMA((WIRES,)),
            pltpu.SemaphoreType.DMA((WIRES,)),
            pltpu.SemaphoreType.DMA((32,)),
        ],
        compiler_params=pltpu.CompilerParams(
            collective_id=0, has_side_effects=True, vmem_limit_bytes=56 * 1024 * 1024
        ),
        cost_estimate=pl.CostEstimate(flops=flops, bytes_accessed=8 << 20, transcendentals=0),
    )(anc_store, block_map, anc_refs, factor1, dinv1, factor2, dinv2, parent, picked)


def solution(mesh):
    return jax.shard_map(
        per_device,
        mesh=mesh,
        in_specs=(
            P("own", None, "col"),
            P(),
            P(),
            P("own", None, "col", None),
            P("own", "col", None),
            P("own", None, "col", None),
            P("own", "col", None),
            P("own"),
            P("own", None),
        ),
        out_specs=(
            P("own", None, "col", None),
            P("own", "col", None),
            P("own", None, "col", None),
            P("own", "col", None),
        ),
        check_vma=False,
    )
```

```python
import functools

import jax
import jax.numpy as jnp
from jax import lax
from jax.experimental import pallas as pl
from jax.experimental.pallas import tpu as pltpu
from jax.sharding import PartitionSpec as P

X, Z, Y = 4, 8, 4
B, A, W = 512, 3, 128
ROWS_A = 64
F32, BF16 = jnp.float32, jnp.bfloat16


class Wires:
    def __init__(self, send_sems, recv_sems):
        self.send_sems, self.recv_sems = send_sems, recv_sems
        self.names, self.sent = {}, []

    def slot(self, name):
        return self.names.setdefault(name, len(self.names))

    def make(self, name, src, dst, device):
        slot = self.slot(name)
        return pltpu.make_async_remote_copy(
            src_ref=src,
            dst_ref=dst,
            send_sem=self.send_sems.at[slot],
            recv_sem=self.recv_sems.at[slot],
            device_id=device,
            device_id_type=pl.DeviceIdType.MESH,
        )

    def send(self, name, src, dst, device):
        copy = self.make(name, src, dst, device)
        copy.start()
        self.sent.append(copy)

    def wait(self, name, dst, device):
        self.make(name, dst, dst, device).wait_recv()

    def finish(self):
        for copy in self.sent:
            copy.wait_send()


WIRES = 256


def dot(a, b):
    return jnp.dot(a, b, preferred_element_type=F32)


def kernel(
    anc, bmap_all, refs_all, f1, dinv1, f2, dinv2, parent_all, picked_all,
    out1, diag1, out2, diag2,
    bmap, parent, picked, store, f1w, f2w, anc_v, stage, refs, low, turned, turned2, cols1, cols2,
    part, dcol, dcolt, dlow, dsend1, dsend2, grow, dinv_v,
    send_sems, recv_sems, local_sems,
):
    own, y = lax.axis_index("own"), lax.axis_index("col")
    core = lax.rem(own, 2)
    chip = own // 2
    x, z = chip // Z, lax.rem(chip, Z)

    def at(dx, dz, dcore=0):
        xx, zz = lax.rem(x + dx + X, X), lax.rem(z + dz + Z, Z)
        return (xx * Z + zz) * 2 + (lax.rem(core + dcore, 2) if dcore else core)

    def yat(d):
        return lax.rem(y + d + Y, Y)

    xup, xdn = (at(1, 0), y), (at(-1, 0), y)
    zup, zdn = (at(0, 1), y), (at(0, -1), y)
    mate = (at(0, 0, 1), y)
    ydev = {d: (own, yat(d)) for d in (1, 2, 3)}
    wires = Wires(send_sems, recv_sems)
    held = {}

    def local(name, src, dst):
        slot = held.setdefault(name, len(held))
        return pltpu.make_async_copy(src, dst, local_sems.at[slot])

    def lanes(index):
        return pl.ds(pl.multiple_of(index * W, W), W)

    barrier = pltpu.get_barrier_semaphore()
    peers = [xup, xdn, zup, zdn, mate, ydev[1], ydev[2], ydev[3]]
    for peer in peers:
        pl.semaphore_signal(barrier, inc=1, device_id=peer, device_id_type=pl.DeviceIdType.MESH)

    load_anc = local("anc", anc, anc_v)
    load_anc.start()
    small = [(refs_all, refs), (bmap_all, bmap), (parent_all, parent), (picked_all, picked)]
    loads = [local(("small", i), src, dst) for i, (src, dst) in enumerate(small)]
    for load in loads:
        load.start()
    load_f1 = local("f1", f1, f1w.at[:, :, lanes(y), :])
    load_f1.start()
    load_f2 = local("f2", f2, f2w.at[:, :, lanes(y), :])
    load_f2.start()
    load_dcol = local("dcol", dinv1.at[:, :, lanes(y)], dcol.at[:, lanes(y), :])
    load_dcol.start()
    load_dinv2 = local("dinv2", dinv2, dinv_v)
    load_dinv2.start()

    load_anc.wait()
    stage[...] = anc_v[...].astype(BF16)
    pl.semaphore_wait(barrier, len(peers))
    mine = pl.ds(own * 2, 2)
    for d in (1, 3, 2):
        wires.send(("t", d), stage.at[:, lanes(yat(d)), :], store.at[mine, :, lanes(y)], ydev[d])
    keep = local("t", stage.at[:, lanes(y), :], store.at[mine, :, lanes(y)])
    keep.start()

    def factor_own(tag, src, dst):
        for m, k in ((0, 1), (1, 0)):
            wires.send((tag, "up", m), src.at[m], dst.at[m, :, lanes(y), :], ydev[1])
            wires.send((tag, "dn", k), src.at[k], dst.at[k, :, lanes(y), :], ydev[3])

    def factor_wait(tag, dst, first):
        for way, d, m in (("up", -1, 0 if first else 1), ("dn", 1, 1 if first else 0)):
            piece = dst.at[m, :, lanes(yat(d)), :]
            wires.wait((tag, way, m), piece, ydev[3 if d == -1 else 1])
            if first:
                wires.send((tag, way, "far"), piece, piece, ydev[1 if d == -1 else 3])

    def factor_far(tag, dst):
        wires.wait((tag, "up", "far"), dst.at[0, :, lanes(yat(2)), :], ydev[3])
        wires.wait((tag, "dn", "far"), dst.at[1, :, lanes(yat(2)), :], ydev[1])

    factor_own("f1", f1, f1w)

    keep.wait()
    for d in (1, 3, 2):
        wires.wait(("t", d), store.at[mine, :, lanes(yat(-d))], ydev[4 - d])

    def chunk(path, dx, dz, slot=None, dcore=0):
        tile = at(dx, dz, dcore) * 2
        tiles = pl.ds(tile, 2) if slot is None else pl.ds(tile + slot, 1)
        rows = pl.ds(0, ROWS_A) if path == "a" else pl.ds(ROWS_A, W - ROWS_A)
        return store.at[tiles, rows, :]

    def share(path, dx, dz, slot=None):
        piece = chunk(path, dx, dz, slot)
        wires.send(("mate", path, dx, dz, slot), piece, piece, mate)
        shared.append((path, dx, dz, slot))

    shared = []
    ZWAY = {"up": (zup, zdn, -1), "dn": (zdn, zup, 1)}
    XWAY = {"up": (xup, xdn, -1), "dn": (xdn, xup, 1)}
    SLOT = {"up": 0, "dn": 1}

    def z_send(path, dx, step, slot=None):
        for way, (to, _, sign) in ZWAY.items():
            half = SLOT[way] if step == 4 else slot
            piece = chunk(path, dx, sign * (step - 1), half)
            wires.send(("z", path, dx, way, step), piece, piece, to)

    def x_send(path, dz):
        piece = chunk(path, 0, dz)
        for way, (to, _, _) in XWAY.items():
            wires.send(("x", path, dz, way, 1), piece, piece, to)

    def z_wait(path, dx, step):
        for way, (to, source, sign) in ZWAY.items():
            half = SLOT[way] if step == 4 else None
            piece = chunk(path, dx, sign * step, half)
            wires.wait(("z", path, dx, way, step), piece, source)
            if step < 4:
                half = SLOT[way] if step == 3 else None
                on = chunk(path, dx, sign * step, half)
                wires.send(("z", path, dx, way, step + 1), on, on, to)
                if path == "b":
                    x_send("b", sign * step)
                share(path, dx, sign * step)
        if step == 4:
            if path == "b":
                x_send("b", 4)
            share(path, dx, 4)

    def x_wait(path, dz):
        for way, (to, source, sign) in XWAY.items():
            piece = chunk(path, sign, dz)
            wires.wait(("x", path, dz, way, 1), piece, source)
            on = chunk(path, sign, dz, SLOT[way])
            wires.send(("x", path, dz, way, 2), on, on, to)
            if path == "a":
                z_send("a", sign, 1)
            share(path, sign, dz)

    def x_far(path, dz):
        for way, (_, source, _) in XWAY.items():
            wires.wait(("x", path, dz, way, 2), chunk(path, 2, dz, SLOT[way]), source)
        if path == "a":
            z_send("a", 2, 1)
        share(path, 2, dz)

    x_send("a", 0)
    z_send("b", 0, 1)
    z_send("a", 0, 1)
    x_send("b", 0)
    share("a", 0, 0)
    share("b", 0, 0)

    x_wait("a", 0)
    z_wait("b", 0, 1)
    x_wait("b", 0)
    z_wait("a", 0, 1)
    x_far("a", 0)
    z_wait("b", 0, 2)
    x_far("b", 0)
    factor_wait("f1", f1w, True)
    x_wait("b", -1)
    z_wait("a", -1, 1)
    x_wait("b", 1)
    z_wait("a", 1, 1)
    x_far("b", -1)
    z_wait("b", 0, 3)
    x_far("b", 1)
    factor_wait("f1", f1w, False)
    factor_own("f2", f2, f2w)
    for d in (1, 3, 2):
        wires.send(("d", d), dinv1.at[:, :, lanes(yat(d))], dcol.at[:, lanes(y), :], ydev[d])
    z_wait("a", 2, 1)
    x_wait("b", -2)
    z_wait("a", 0, 2)
    x_wait("b", 2)
    z_wait("b", 0, 4)
    x_far("b", -2)
    x_far("b", 2)
    z_wait("a", -1, 2)
    factor_far("f1", f1w)
    x_wait("b", -3)
    z_wait("a", 1, 2)
    x_wait("b", 3)
    z_wait("a", 2, 2)
    x_far("b", -3)
    x_far("b", 3)
    factor_wait("f2", f2w, True)
    z_wait("a", 0, 3)
    x_wait("b", 4)
    z_wait("a", -1, 3)
    x_far("b", 4)
    z_wait("a", 1, 3)
    z_wait("a", 2, 3)
    for dx in (0, -1, 1, 2):
        z_wait("a", dx, 4)
    for path, dx, dz, slot in shared:
        wires.wait(("mate", path, dx, dz, slot), chunk(path, dx, dz, slot, 1), mate)
    for load in loads:
        load.wait()
    load_f1.wait()

    def tile(m, i, k):
        return store[bmap[refs[i, k, own * 2 + m]]]

    def stacked(parts):
        return jnp.concatenate(parts, axis=0)

    def give_columns(tag, turned_ref, cols_ref, m):
        for d in (1, 3, 2):
            wires.send(
                (tag, m, d), turned_ref.at[yat(d), m], cols_ref.at[m, :, :, lanes(y)], ydev[d]
            )
        own_part = local((tag, m), turned_ref.at[y, m], cols_ref.at[m, :, :, lanes(y)])
        own_part.start()
        return own_part

    def take_columns(tag, cols_ref, m, own_part):
        own_part.wait()
        for d in (1, 3, 2):
            wires.wait((tag, m, d), cols_ref.at[m, :, :, lanes(yat(-d))], ydev[4 - d])

    def spread(acc, m, n, out_ref, turned_ref, low_ref):
        for i in range(A):
            rows = acc[i * W : (i + 1) * W]
            out_ref[m, i, :, n * 256 : (n + 1) * 256] = rows
            if low_ref is not None:
                low_ref[m, i, :, n * 256 : (n + 1) * 256] = rows.astype(BF16)
            for b in range(2):
                turned_ref[2 * n + b, m, i] = rows[:, b * W : (b + 1) * W].T.astype(BF16)

    kept1 = []
    for m in range(2):
        for n in range(2):
            acc = 0.0
            for k in range(A):
                acc += dot(
                    stacked([tile(m, i, k) for i in range(A)]), f1w[m, k, :, n * 256 : (n + 1) * 256]
                )
            spread(-acc, m, n, out1, turned, low)
        kept1.append(give_columns("c1", turned, cols1, m))

    factor_wait("f2", f2w, False)
    factor_far("f2", f2w)
    load_f2.wait()
    for m in range(2):
        p = parent[m]
        q = [picked[m, 0], picked[m, 1]]
        for n in range(2):
            acc = 0.0
            for k in range(2):
                acc += dot(
                    stacked([tile(p, q[i], q[k]) for i in range(2)]),
                    f2w[m, k + 1, :, n * 256 : (n + 1) * 256],
                )
            part[m, :, n * 256 : (n + 1) * 256] = acc
    load_dcol.wait()
    for d in (1, 3, 2):
        wires.wait(("d", d), dcol.at[:, lanes(yat(-d)), :], ydev[4 - d])
    for m in range(2):
        for b in range(Y):
            dcolt[m, :, b * W : (b + 1) * W] = dcol[m, b * W : (b + 1) * W, :].T

    def corrections(cols_ref, fw, m):
        return sum(dot(cols_ref[m, k], fw[m, k]) for k in range(A))

    def give_rows(tag, src, dst, m):
        for d in (1, 3, 2):
            wires.send((tag, m, d), src.at[yat(d), m], dst.at[m, :, lanes(y)], ydev[d])
        own_part = local((tag, m), src.at[y, m], dst.at[m, :, lanes(y)])
        own_part.start()
        return own_part

    def take_rows(tag, dst, m, own_part):
        own_part.wait()
        for d in (1, 3, 2):
            wires.wait((tag, m, d), dst.at[m, :, lanes(yat(-d))], ydev[4 - d])

    kept_diag = []
    for m in range(2):
        take_columns("c1", cols1, m, kept1[m])
        turned_diag = dcolt[m] - corrections(cols1, f1w, m)
        dlow[m] = turned_diag.astype(BF16)
        for b in range(Y):
            dsend1[b, m] = turned_diag[:, b * W : (b + 1) * W].T
        kept_diag.append(give_rows("g1", dsend1, diag1, m))

    kept2 = []
    for m in range(2):
        p = parent[m]
        q = [picked[m, 0], picked[m, 1]]
        for n in range(2):
            span = slice(n * 256, (n + 1) * 256)
            acc = dot(stacked([dlow[p], low[p, q[0]], low[p, q[1]]]), f2w[m, 0, :, span])
            top = dot(cols1[p, q[0]], f2w[m, 1, :, span]) + dot(cols1[p, q[1]], f2w[m, 2, :, span])
            acc += stacked([top, part[m, :, span]])
            spread(-acc, m, n, out2, turned2, None)
        kept2.append(give_columns("c2", turned2, cols2, m))
    load_dinv2.wait()
    kept_grow = []
    for m in range(2):
        take_columns("c2", cols2, m, kept2[m])
        correction = corrections(cols2, f2w, m)
        for b in range(Y):
            dsend2[b, m] = correction[:, b * W : (b + 1) * W].T
        kept_grow.append(give_rows("g2", dsend2, grow, m))
    for m in range(2):
        take_rows("g1", diag1, m, kept_diag[m])
    for m in range(2):
        take_rows("g2", grow, m, kept_grow[m])
        diag2[m] = dinv_v[m] - grow[m]
    wires.finish()


def write_out(*refs):
    sources, results, sems = refs[:4], refs[4:8], refs[8]
    copies = [pltpu.make_async_copy(a, b, sems.at[i]) for i, (a, b) in enumerate(zip(sources, results))]
    for copy in copies:
        copy.start()
    for copy in copies:
        copy.wait()


def per_device(anc_store, block_map, anc_refs, factor1, dinv1, factor2, dinv2, parent, picked):
    any_space = pl.BlockSpec(memory_space=pl.ANY)
    vmem = pl.BlockSpec(memory_space=pltpu.VMEM)
    operands = (
        anc_store, block_map, anc_refs.transpose(1, 2, 0), factor1, dinv1, factor2, dinv2, parent, picked
    )
    flops = 2 * 2 * 2 * (9 + 3) * W * B * B
    shapes = ((2, A, W, B), (2, W, B), (2, A, W, B), (2, W, B))
    results = pl.pallas_call(
        kernel,
        out_shape=tuple(pltpu.VMEM(shape, F32) for shape in shapes),
        in_specs=[any_space] * 9,
        out_specs=(vmem,) * 4,
        scratch_shapes=[
            pltpu.SMEM((2 * X * Z * 2,), jnp.int32),
            pltpu.SMEM((2,), jnp.int32),
            pltpu.SMEM((2, 2), jnp.int32),
            pltpu.VMEM((X * Z * 4, W, B), BF16),
            pltpu.VMEM((2, A, B, B), BF16),
            pltpu.VMEM((2, A, B, B), BF16),
            pltpu.VMEM((2, B, W), F32),
            pltpu.VMEM((2, B, W), BF16),
            pltpu.SMEM((A, A, 2 * X * Z * 2), jnp.int32),
            pltpu.VMEM((2, A, W, B), BF16),
            pltpu.VMEM((Y, 2, A, W, W), BF16),
            pltpu.VMEM((Y, 2, A, W, W), BF16),
            pltpu.VMEM((2, A, W, B), BF16),
            pltpu.VMEM((2, A, W, B), BF16),
            pltpu.VMEM((2, 2 * W, B), F32),
            pltpu.VMEM((2, B, W), F32),
            pltpu.VMEM((2, W, B), F32),
            pltpu.VMEM((2, W, B), BF16),
            pltpu.VMEM((Y, 2, W, W), F32),
            pltpu.VMEM((Y, 2, W, W), F32),
            pltpu.VMEM((2, W, B), F32),
            pltpu.VMEM((2, W, B), F32),
            pltpu.SemaphoreType.DMA((WIRES,)),
            pltpu.SemaphoreType.DMA((WIRES,)),
            pltpu.SemaphoreType.DMA((32,)),
        ],
        compiler_params=pltpu.CompilerParams(
            collective_id=0, has_side_effects=True, vmem_limit_bytes=44 * 1024 * 1024
        ),
        cost_estimate=pl.CostEstimate(flops=flops, bytes_accessed=8 << 20, transcendentals=0),
    )(*(pltpu.with_memory_space_constraint(operand, pltpu.HBM) for operand in operands))
    return pl.pallas_call(
        write_out,
        out_shape=tuple(jax.ShapeDtypeStruct(shape, F32) for shape in shapes),
        in_specs=[vmem] * 4,
        out_specs=(any_space,) * 4,
        scratch_shapes=[pltpu.SemaphoreType.DMA((4,))],
        compiler_params=pltpu.CompilerParams(vmem_limit_bytes=4 * 1024 * 1024),
        cost_estimate=pl.CostEstimate(flops=0, bytes_accessed=8 << 20, transcendentals=0),
    )(*(pltpu.with_memory_space_constraint(result, pltpu.VMEM) for result in results))


def solution(mesh):
    return jax.shard_map(
        per_device,
        mesh=mesh,
        in_specs=(
            P("own", None, "col"),
            P(),
            P(),
            P("own", None, "col", None),
            P("own", "col", None),
            P("own", None, "col", None),
            P("own", "col", None),
            P("own"),
            P("own", None),
        ),
        out_specs=(
            P("own", None, "col", None),
            P("own", "col", None),
            P("own", None, "col", None),
            P("own", "col", None),
        ),
        check_vma=False,
    )
```

```python
import functools

import jax
import jax.numpy as jnp
from jax import lax
from jax.experimental import pallas as pl
from jax.experimental.pallas import tpu as pltpu
from jax.sharding import PartitionSpec as P

X, Z, Y = 4, 8, 4
B, A, W = 512, 3, 128
ROWS_A = 48
F32, BF16 = jnp.float32, jnp.bfloat16
ORDER = (
    ("x", "a", 0, 1), ("z", "b", 0, 1), ("f", "1", 0, 1), ("x", "b", 0, 1), ("z", "a", 0, 1),
    ("x", "a", 0, 2), ("z", "a", -1, 1), ("z", "a", 1, 1), ("x", "b", -1, 1), ("z", "b", 0, 2),
    ("x", "b", 1, 1), ("f", "1", 0, 2), ("x", "b", 0, 2), ("z", "a", 0, 2), ("x", "b", -1, 2),
    ("z", "a", 2, 1), ("z", "a", -1, 2), ("x", "b", -2, 1), ("z", "a", 1, 2), ("x", "b", 2, 1),
    ("z", "b", 0, 3), ("f", "1", 0, 3), ("x", "b", 1, 2), ("z", "a", 0, 3), ("x", "b", -2, 2),
    ("x", "b", 2, 2), ("z", "a", 2, 2), ("z", "a", -1, 3), ("x", "b", -3, 1), ("f", "2", 0, 1),
    ("z", "a", 1, 3), ("z", "b", 0, 4), ("x", "b", 3, 1), ("z", "a", 0, 4), ("x", "b", -3, 2),
    ("z", "a", 2, 3), ("z", "a", -1, 4), ("z", "a", 1, 4), ("x", "b", 4, 1), ("z", "a", 2, 4),
    ("x", "b", 3, 2), ("x", "b", 4, 2),
)


class Wires:
    def __init__(self, send_sems, recv_sems):
        self.send_sems, self.recv_sems = send_sems, recv_sems
        self.names, self.sent = {}, []

    def slot(self, name):
        return self.names.setdefault(name, len(self.names))

    def make(self, name, src, dst, device):
        slot = self.slot(name)
        return pltpu.make_async_remote_copy(
            src_ref=src,
            dst_ref=dst,
            send_sem=self.send_sems.at[slot],
            recv_sem=self.recv_sems.at[slot],
            device_id=device,
            device_id_type=pl.DeviceIdType.MESH,
        )

    def send(self, name, src, dst, device):
        copy = self.make(name, src, dst, device)
        copy.start()
        self.sent.append(copy)

    def wait(self, name, dst, device):
        self.make(name, dst, dst, device).wait_recv()

    def finish(self):
        for copy in self.sent:
            copy.wait_send()


WIRES = 256


def dot(a, b):
    return jnp.dot(a, b, preferred_element_type=F32)


def kernel(
    anc, bmap_all, refs_all, f1, dinv1, f2, dinv2, parent_all, picked_all,
    out1, diag1, out2, diag2,
    bmap, parent, picked, store, f1w, f2w, anc_v, stage, refs, low, low2, turned, cols1, part,
    dinv1_v, dinv2_v, dstage, dcolt, dlow, f2t, gsend, grow1, psum, psend, grow2,
    send_sems, recv_sems, local_sems,
):
    own, y = lax.axis_index("own"), lax.axis_index("col")
    core = lax.rem(own, 2)
    chip = own // 2
    x, z = chip // Z, lax.rem(chip, Z)

    def at(dx, dz, dcore=0):
        xx, zz = lax.rem(x + dx + X, X), lax.rem(z + dz + Z, Z)
        return (xx * Z + zz) * 2 + (lax.rem(core + dcore, 2) if dcore else core)

    def yat(d):
        return lax.rem(y + d + Y, Y)

    xup, xdn = (at(1, 0), y), (at(-1, 0), y)
    zup, zdn = (at(0, 1), y), (at(0, -1), y)
    mate = (at(0, 0, 1), y)
    ydev = {d: (own, yat(d)) for d in (1, 2, 3)}
    wires = Wires(send_sems, recv_sems)
    held = {}

    def local(name, src, dst):
        slot = held.setdefault(name, len(held))
        return pltpu.make_async_copy(src, dst, local_sems.at[slot])

    def lanes(index):
        return pl.ds(pl.multiple_of(index * W, W), W)

    barrier = pltpu.get_barrier_semaphore()
    peers = [xup, xdn, zup, zdn, mate, ydev[1], ydev[2], ydev[3]]
    for peer in peers:
        pl.semaphore_signal(barrier, inc=1, device_id=peer, device_id_type=pl.DeviceIdType.MESH)

    load_anc = local("anc", anc, anc_v)
    load_anc.start()
    small = [(refs_all, refs), (bmap_all, bmap), (parent_all, parent), (picked_all, picked)]
    loads = [local(("small", i), src, dst) for i, (src, dst) in enumerate(small)]
    for load in loads:
        load.start()
    load_f1 = local("f1", f1, f1w.at[:, :, lanes(y), :])
    load_f1.start()
    load_f2 = local("f2", f2, f2w.at[:, :, lanes(y), :])
    load_f2.start()
    load_dinv1 = local("dinv1", dinv1, dinv1_v)
    load_dinv1.start()
    load_dinv2 = local("dinv2", dinv2, dinv2_v)
    load_dinv2.start()

    load_anc.wait()
    stage[...] = anc_v[...].astype(BF16)
    pl.semaphore_wait(barrier, len(peers))
    mine = pl.ds(own * 2, 2)
    for d in (1, 3, 2):
        wires.send(("t", d), stage.at[:, lanes(yat(d)), :], store.at[mine, :, lanes(y)], ydev[d])
    keep = local("t", stage.at[:, lanes(y), :], store.at[mine, :, lanes(y)])
    keep.start()

    def factor_own(tag, src, dst):
        for m, k in ((0, 1), (1, 0)):
            wires.send((tag, "up", m), src.at[m], dst.at[m, :, lanes(y), :], ydev[1])
            wires.send((tag, "dn", k), src.at[k], dst.at[k, :, lanes(y), :], ydev[3])

    def factor_wait(tag, dst, first):
        for way, d, m in (("up", -1, 0 if first else 1), ("dn", 1, 1 if first else 0)):
            piece = dst.at[m, :, lanes(yat(d)), :]
            wires.wait((tag, way, m), piece, ydev[3 if d == -1 else 1])
            if first:
                wires.send((tag, way, "far"), piece, piece, ydev[1 if d == -1 else 3])

    def factor_far(tag, dst):
        wires.wait((tag, "up", "far"), dst.at[0, :, lanes(yat(2)), :], ydev[3])
        wires.wait((tag, "dn", "far"), dst.at[1, :, lanes(yat(2)), :], ydev[1])

    factor_own("f1", f1, f1w)

    load_dinv1.wait()
    for m in range(2):
        for b in range(Y):
            dstage[b, m] = dinv1_v[m, :, b * W : (b + 1) * W].T.astype(BF16)
    for d in (1, 3, 2):
        wires.send(("d", d), dstage.at[yat(d)], dcolt.at[:, :, lanes(y)], ydev[d])
    keep_d = local("d", dstage.at[y], dcolt.at[:, :, lanes(y)])
    keep_d.start()

    keep.wait()
    for d in (1, 3, 2):
        wires.wait(("t", d), store.at[mine, :, lanes(yat(-d))], ydev[4 - d])

    def chunk(path, dx, dz, slot=None, dcore=0):
        tile = at(dx, dz, dcore) * 2
        tiles = pl.ds(tile, 2) if slot is None else pl.ds(tile + slot, 1)
        rows = pl.ds(0, ROWS_A) if path == "a" else pl.ds(ROWS_A, W - ROWS_A)
        return store.at[tiles, rows, :]

    def share(path, dx, dz, slot=None):
        piece = chunk(path, dx, dz, slot)
        wires.send(("mate", path, dx, dz, slot), piece, piece, mate)
        shared.append((path, dx, dz, slot))

    shared = []
    ZWAY = {"up": (zup, zdn, -1), "dn": (zdn, zup, 1)}
    XWAY = {"up": (xup, xdn, -1), "dn": (xdn, xup, 1)}
    SLOT = {"up": 0, "dn": 1}

    def z_send(path, dx, step, slot=None):
        for way, (to, _, sign) in ZWAY.items():
            half = SLOT[way] if step == 4 else slot
            piece = chunk(path, dx, sign * (step - 1), half)
            wires.send(("z", path, dx, way, step), piece, piece, to)

    def x_send(path, dz):
        piece = chunk(path, 0, dz)
        for way, (to, _, _) in XWAY.items():
            wires.send(("x", path, dz, way, 1), piece, piece, to)

    def z_wait(path, dx, step):
        for way, (to, source, sign) in ZWAY.items():
            half = SLOT[way] if step == 4 else None
            piece = chunk(path, dx, sign * step, half)
            wires.wait(("z", path, dx, way, step), piece, source)
            if step < 4:
                half = SLOT[way] if step == 3 else None
                on = chunk(path, dx, sign * step, half)
                wires.send(("z", path, dx, way, step + 1), on, on, to)
                if path == "b":
                    x_send("b", sign * step)
                share(path, dx, sign * step)
        if step == 4:
            if path == "b":
                x_send("b", 4)
            share(path, dx, 4)

    def x_wait(path, dz):
        for way, (to, source, sign) in XWAY.items():
            piece = chunk(path, sign, dz)
            wires.wait(("x", path, dz, way, 1), piece, source)
            on = chunk(path, sign, dz, SLOT[way])
            wires.send(("x", path, dz, way, 2), on, on, to)
            if path == "a":
                z_send("a", sign, 1)
            share(path, sign, dz)

    def x_far(path, dz):
        for way, (_, source, _) in XWAY.items():
            wires.wait(("x", path, dz, way, 2), chunk(path, 2, dz, SLOT[way]), source)
        if path == "a":
            z_send("a", 2, 1)
        share(path, 2, dz)

    x_send("a", 0)
    z_send("b", 0, 1)
    z_send("a", 0, 1)
    x_send("b", 0)
    share("a", 0, 0)
    share("b", 0, 0)

    load_f2.wait()
    for m in range(2):
        for k in range(A):
            f2t[m, :, k * W : (k + 1) * W] = f2w[m, k, lanes(y), :].T

    for kind, tag, offset, step in ORDER:
        if kind == "z":
            z_wait(tag, offset, step)
        elif kind == "x":
            (x_wait if step == 1 else x_far)(tag, offset)
        elif tag == "2":
            factor_wait("f2", f2w, True)
        elif step == 3:
            factor_far("f1", f1w)
        else:
            factor_wait("f1", f1w, step == 1)
            if step == 2:
                factor_own("f2", f2, f2w)
    for path, dx, dz, slot in shared:
        wires.wait(("mate", path, dx, dz, slot), chunk(path, dx, dz, slot, 1), mate)
    for load in loads:
        load.wait()
    load_f1.wait()

    def tile(m, i, k):
        return store[bmap[refs[i, k, own * 2 + m]]]

    def stacked(parts):
        return jnp.concatenate(parts, axis=0)

    def give_columns(tag, turned_ref, cols_ref, m):
        for d in (1, 3, 2):
            wires.send(
                (tag, m, d), turned_ref.at[yat(d), m], cols_ref.at[m, :, :, lanes(y)], ydev[d]
            )
        own_part = local((tag, m), turned_ref.at[y, m], cols_ref.at[m, :, :, lanes(y)])
        own_part.start()
        return own_part

    def take_columns(tag, cols_ref, m, own_part):
        own_part.wait()
        for d in (1, 3, 2):
            wires.wait((tag, m, d), cols_ref.at[m, :, :, lanes(yat(-d))], ydev[4 - d])

    def spread(acc, m, first, n, out_ref, low_ref, turned_ref=None):
        for i in range(first, first + acc.shape[0] // W):
            rows = acc[(i - first) * W : (i - first + 1) * W]
            out_ref[m, i, :, n * 256 : (n + 1) * 256] = rows
            low_ref[m, i, :, n * 256 : (n + 1) * 256] = rows.astype(BF16)
            if turned_ref is not None:
                for b in range(2):
                    turned_ref[2 * n + b, m, i] = rows[:, b * W : (b + 1) * W].T.astype(BF16)

    kept1 = []
    for m in range(2):
        for n in range(2):
            acc = 0.0
            for k in range(A):
                acc += dot(
                    stacked([tile(m, i, k) for i in range(A)]), f1w[m, k, :, n * 256 : (n + 1) * 256]
                )
            spread(-acc, m, 0, n, out1, low, turned)
        kept1.append(give_columns("c1", turned, cols1, m))

    factor_wait("f2", f2w, False)
    factor_far("f2", f2w)
    for m in range(2):
        p = parent[m]
        q = [picked[m, 0], picked[m, 1]]
        for n in range(2):
            span = slice(n * 256, (n + 1) * 256)
            acc = dot(stacked([low[p, q[0]], low[p, q[1]]]), f2w[m, 0, :, span])
            for k in range(2):
                acc += dot(stacked([tile(p, q[i], q[k]) for i in range(2)]), f2w[m, k + 1, :, span])
            spread(-acc, m, 1, n, out2, low2)
            part[m, :, span] = dot(f2t[m, :, W:], stacked([low2[m, 1, :, span], low2[m, 2, :, span]]))
    keep_d.wait()
    for d in (1, 3, 2):
        wires.wait(("d", d), dcolt.at[:, :, lanes(yat(-d))], ydev[4 - d])

    def corrections(cols_ref, fw, m):
        return sum(dot(cols_ref[m, k], fw[m, k]) for k in range(A))

    def give_rows(tag, src, dst, m):
        for d in (1, 3, 2):
            wires.send((tag, m, d), src.at[yat(d), m], dst.at[m, :, lanes(y)], ydev[d])
        own_part = local((tag, m), src.at[y, m], dst.at[m, :, lanes(y)])
        own_part.start()
        return own_part

    def take_rows(tag, dst, m, own_part):
        own_part.wait()
        for d in (1, 3, 2):
            wires.wait((tag, m, d), dst.at[m, :, lanes(yat(-d))], ydev[4 - d])

    kept_diag = []
    for m in range(2):
        take_columns("c1", cols1, m, kept1[m])
        turned_diag = corrections(cols1, f1w, m)
        dlow[m] = (dcolt[m].astype(F32) - turned_diag).astype(BF16)
        for b in range(Y):
            gsend[b, m] = turned_diag[:, b * W : (b + 1) * W].T.astype(BF16)
        kept_diag.append(give_rows("g1", gsend, grow1, m))

    for m in range(2):
        p = parent[m]
        q = [picked[m, 0], picked[m, 1]]
        for n in range(2):
            span = slice(n * 256, (n + 1) * 256)
            acc = dot(dlow[p], f2w[m, 0, :, span])
            acc += dot(cols1[p, q[0]], f2w[m, 1, :, span]) + dot(cols1[p, q[1]], f2w[m, 2, :, span])
            spread(-acc, m, 0, n, out2, low2)
            term = part[m, :, span] + dot(f2t[m, :, :W], low2[m, 0, :, span])
            for b in range(Y):
                rows = term[b * W : (b + 1) * W]
                psum[m, b, :, span] = rows
                psend[m, b, :, span] = rows.astype(BF16)
        for d in (1, 3, 2):
            wires.send(("g2", m, d), psend.at[m, yat(d)], grow2.at[m, d - 1], ydev[d])
    for m in range(2):
        take_rows("g1", grow1, m, kept_diag[m])
        diag1[m] = dinv1_v[m] - grow1[m].astype(F32)
    load_dinv2.wait()
    for m in range(2):
        total = psum[m, y]
        for d in (1, 3, 2):
            wires.wait(("g2", m, d), grow2.at[m, d - 1], ydev[4 - d])
        for d in (1, 2, 3):
            total += grow2[m, d - 1].astype(F32)
        diag2[m] = dinv2_v[m] - total
    wires.finish()


def write_out(*refs):
    sources, results, sems = refs[:4], refs[4:8], refs[8]
    copies = [pltpu.make_async_copy(a, b, sems.at[i]) for i, (a, b) in enumerate(zip(sources, results))]
    for copy in copies:
        copy.start()
    for copy in copies:
        copy.wait()


def per_device(anc_store, block_map, anc_refs, factor1, dinv1, factor2, dinv2, parent, picked):
    any_space = pl.BlockSpec(memory_space=pl.ANY)
    vmem = pl.BlockSpec(memory_space=pltpu.VMEM)
    operands = (
        anc_store, block_map, anc_refs.transpose(1, 2, 0), factor1, dinv1, factor2, dinv2, parent, picked
    )
    flops = 2 * 2 * 2 * (9 + 3) * W * B * B
    shapes = ((2, A, W, B), (2, W, B), (2, A, W, B), (2, W, B))
    results = pl.pallas_call(
        kernel,
        out_shape=tuple(pltpu.VMEM(shape, F32) for shape in shapes),
        in_specs=[any_space] * 9,
        out_specs=(vmem,) * 4,
        scratch_shapes=[
            pltpu.SMEM((2 * X * Z * 2,), jnp.int32),
            pltpu.SMEM((2,), jnp.int32),
            pltpu.SMEM((2, 2), jnp.int32),
            pltpu.VMEM((X * Z * 4, W, B), BF16),
            pltpu.VMEM((2, A, B, B), BF16),
            pltpu.VMEM((2, A, B, B), BF16),
            pltpu.VMEM((2, B, W), F32),
            pltpu.VMEM((2, B, W), BF16),
            pltpu.SMEM((A, A, 2 * X * Z * 2), jnp.int32),
            pltpu.VMEM((2, A, W, B), BF16),
            pltpu.VMEM((2, A, W, B), BF16),
            pltpu.VMEM((Y, 2, A, W, W), BF16),
            pltpu.VMEM((2, A, W, B), BF16),
            pltpu.VMEM((2, B, B), F32),
            pltpu.VMEM((2, W, B), F32),
            pltpu.VMEM((2, W, B), F32),
            pltpu.VMEM((Y, 2, W, W), BF16),
            pltpu.VMEM((2, W, B), BF16),
            pltpu.VMEM((2, W, B), BF16),
            pltpu.VMEM((2, B, A * W), BF16),
            pltpu.VMEM((Y, 2, W, W), BF16),
            pltpu.VMEM((2, W, B), BF16),
            pltpu.VMEM((2, Y, W, B), F32),
            pltpu.VMEM((2, Y, W, B), BF16),
            pltpu.VMEM((2, 3, W, B), BF16),
            pltpu.SemaphoreType.DMA((WIRES,)),
            pltpu.SemaphoreType.DMA((WIRES,)),
            pltpu.SemaphoreType.DMA((32,)),
        ],
        compiler_params=pltpu.CompilerParams(
            collective_id=0, has_side_effects=True, vmem_limit_bytes=44 * 1024 * 1024
        ),
        cost_estimate=pl.CostEstimate(flops=flops, bytes_accessed=8 << 20, transcendentals=0),
    )(*(pltpu.with_memory_space_constraint(operand, pltpu.HBM) for operand in operands))
    return pl.pallas_call(
        write_out,
        out_shape=tuple(jax.ShapeDtypeStruct(shape, F32) for shape in shapes),
        in_specs=[vmem] * 4,
        out_specs=(any_space,) * 4,
        scratch_shapes=[pltpu.SemaphoreType.DMA((4,))],
        compiler_params=pltpu.CompilerParams(vmem_limit_bytes=4 * 1024 * 1024),
        cost_estimate=pl.CostEstimate(flops=0, bytes_accessed=8 << 20, transcendentals=0),
    )(*(pltpu.with_memory_space_constraint(result, pltpu.VMEM) for result in results))


def solution(mesh):
    return jax.shard_map(
        per_device,
        mesh=mesh,
        in_specs=(
            P("own", None, "col"),
            P(),
            P(),
            P("own", None, "col", None),
            P("own", "col", None),
            P("own", None, "col", None),
            P("own", "col", None),
            P("own"),
            P("own", None),
        ),
        out_specs=(
            P("own", None, "col", None),
            P("own", "col", None),
            P("own", None, "col", None),
            P("own", "col", None),
        ),
        check_vma=False,
    )
```

```python
import functools

import jax
import jax.numpy as jnp
from jax import lax
from jax.experimental import pallas as pl
from jax.experimental.pallas import tpu as pltpu
from jax.sharding import PartitionSpec as P

X, Z, Y = 4, 8, 4
B, A, W = 512, 3, 128
ROWS_A = 48
F32, BF16 = jnp.float32, jnp.bfloat16
ORDER = (
    ("x", "a", 0, 1), ("z", "b", 0, 1), ("x", "b", 0, 1), ("z", "a", 0, 1), ("x", "a", 0, 2),
    ("z", "a", -1, 1), ("f", "1", 0, 1), ("z", "a", 1, 1), ("x", "b", -1, 1), ("z", "b", 0, 2),
    ("x", "b", 1, 1), ("x", "b", 0, 2), ("f", "1", 0, 2), ("z", "a", 0, 2), ("x", "b", -1, 2),
    ("z", "a", 2, 1), ("z", "a", -1, 2), ("x", "b", -2, 1), ("z", "a", 1, 2), ("x", "b", 2, 1),
    ("z", "b", 0, 3), ("x", "b", 1, 2), ("f", "1", 0, 3), ("z", "a", 0, 3), ("x", "b", -2, 2),
    ("x", "b", 2, 2), ("z", "a", 2, 2), ("z", "a", -1, 3), ("f", "2", 0, 1), ("x", "b", -3, 1),
    ("z", "a", 1, 3), ("z", "b", 0, 4), ("x", "b", 3, 1), ("z", "a", 0, 4), ("x", "b", -3, 2),
    ("z", "a", 2, 3), ("z", "a", -1, 4), ("z", "a", 1, 4), ("x", "b", 4, 1), ("z", "a", 2, 4),
    ("x", "b", 3, 2), ("x", "b", 4, 2),
)


class Wires:
    def __init__(self, send_sems, recv_sems):
        self.send_sems, self.recv_sems = send_sems, recv_sems
        self.names, self.sent = {}, []

    def slot(self, name):
        return self.names.setdefault(name, len(self.names))

    def make(self, name, src, dst, device):
        slot = self.slot(name)
        return pltpu.make_async_remote_copy(
            src_ref=src,
            dst_ref=dst,
            send_sem=self.send_sems.at[slot],
            recv_sem=self.recv_sems.at[slot],
            device_id=device,
            device_id_type=pl.DeviceIdType.MESH,
        )

    def send(self, name, src, dst, device):
        copy = self.make(name, src, dst, device)
        copy.start()
        self.sent.append(copy)

    def wait(self, name, dst, device):
        self.make(name, dst, dst, device).wait_recv()

    def finish(self):
        for copy in self.sent:
            copy.wait_send()


WIRES = 256


def dot(a, b):
    return jnp.dot(a, b, preferred_element_type=F32)


def kernel(
    anc, bmap_all, refs_all, f1, dinv1, f2, dinv2, parent_all, picked_all,
    out1, diag1, out2, diag2,
    bmap, parent, picked, store, f1w, f2w, anc_v, stage, refs, low, low2, turned, cols1, part,
    dinv1_v, dinv2_v, dstage, dcolt, dlow, f2t, gsend, grow1, psum, psend, grow2,
    send_sems, recv_sems, local_sems,
):
    own, y = lax.axis_index("own"), lax.axis_index("col")
    core = lax.rem(own, 2)
    chip = own // 2
    x, z = chip // Z, lax.rem(chip, Z)

    def at(dx, dz, dcore=0):
        xx, zz = lax.rem(x + dx + X, X), lax.rem(z + dz + Z, Z)
        return (xx * Z + zz) * 2 + (lax.rem(core + dcore, 2) if dcore else core)

    def yat(d):
        return lax.rem(y + d + Y, Y)

    xup, xdn = (at(1, 0), y), (at(-1, 0), y)
    zup, zdn = (at(0, 1), y), (at(0, -1), y)
    mate = (at(0, 0, 1), y)
    ydev = {d: (own, yat(d)) for d in (1, 2, 3)}
    wires = Wires(send_sems, recv_sems)
    held = {}

    def local(name, src, dst):
        slot = held.setdefault(name, len(held))
        return pltpu.make_async_copy(src, dst, local_sems.at[slot])

    def lanes(index):
        return pl.ds(pl.multiple_of(index * W, W), W)

    barrier = pltpu.get_barrier_semaphore()
    peers = [xup, xdn, zup, zdn, mate, ydev[1], ydev[2], ydev[3]]
    for peer in peers:
        pl.semaphore_signal(barrier, inc=1, device_id=peer, device_id_type=pl.DeviceIdType.MESH)

    load_anc = local("anc", anc, anc_v)
    load_anc.start()
    small = [(refs_all, refs), (bmap_all, bmap), (parent_all, parent), (picked_all, picked)]
    loads = [local(("small", i), src, dst) for i, (src, dst) in enumerate(small)]
    for load in loads:
        load.start()
    load_f1 = local("f1", f1, f1w.at[:, :, lanes(y), :])
    load_f1.start()
    load_f2 = local("f2", f2, f2w.at[:, :, lanes(y), :])
    load_f2.start()
    load_dinv1 = local("dinv1", dinv1, dinv1_v)
    load_dinv1.start()
    load_dinv2 = local("dinv2", dinv2, dinv2_v)
    load_dinv2.start()

    load_anc.wait()
    stage[...] = anc_v[...].astype(BF16)
    pl.semaphore_wait(barrier, len(peers))
    mine = pl.ds(own * 2, 2)
    for d in (1, 3, 2):
        wires.send(("t", d), stage.at[:, lanes(yat(d)), :], store.at[mine, :, lanes(y)], ydev[d])
    keep = local("t", stage.at[:, lanes(y), :], store.at[mine, :, lanes(y)])
    keep.start()

    def factor_own(tag, src, dst, m):
        wires.send((tag, "up", m), src.at[m], dst.at[m, :, lanes(y), :], ydev[1])
        wires.send((tag, "dn", 1 - m), src.at[1 - m], dst.at[1 - m, :, lanes(y), :], ydev[3])

    def factor_wait(tag, dst, first):
        for way, d, m in (("up", -1, 0 if first else 1), ("dn", 1, 1 if first else 0)):
            piece = dst.at[m, :, lanes(yat(d)), :]
            wires.wait((tag, way, m), piece, ydev[3 if d == -1 else 1])
            if first:
                wires.send((tag, way, "far"), piece, piece, ydev[1 if d == -1 else 3])

    def factor_far(tag, dst):
        wires.wait((tag, "up", "far"), dst.at[0, :, lanes(yat(2)), :], ydev[3])
        wires.wait((tag, "dn", "far"), dst.at[1, :, lanes(yat(2)), :], ydev[1])

    load_dinv1.wait()
    for m in range(2):
        for b in range(Y):
            dstage[b, m] = dinv1_v[m, :, b * W : (b + 1) * W].T.astype(BF16)
    factor_own("f1", f1, f1w, 0)
    keep_d = local("d", dstage.at[y], dcolt.at[:, :, lanes(y)])
    keep_d.start()

    keep.wait()
    for d in (1, 3, 2):
        wires.wait(("t", d), store.at[mine, :, lanes(yat(-d))], ydev[4 - d])

    def chunk(path, dx, dz, slot=None, dcore=0):
        tile = at(dx, dz, dcore) * 2
        tiles = pl.ds(tile, 2) if slot is None else pl.ds(tile + slot, 1)
        rows = pl.ds(0, ROWS_A) if path == "a" else pl.ds(ROWS_A, W - ROWS_A)
        return store.at[tiles, rows, :]

    def share(path, dx, dz, slot=None):
        piece = chunk(path, dx, dz, slot)
        wires.send(("mate", path, dx, dz, slot), piece, piece, mate)
        shared.append((path, dx, dz, slot))

    shared = []
    ZWAY = {"up": (zup, zdn, -1), "dn": (zdn, zup, 1)}
    XWAY = {"up": (xup, xdn, -1), "dn": (xdn, xup, 1)}
    SLOT = {"up": 0, "dn": 1}

    def z_send(path, dx, step):
        for slot in range(2):
            for way, (to, _, sign) in ZWAY.items():
                piece = chunk(path, dx, sign * (step - 1), slot)
                wires.send(("z", path, dx, way, step, slot), piece, piece, to)

    def x_send(path, dz):
        for slot in range(2):
            for way, (to, _, _) in XWAY.items():
                piece = chunk(path, 0, dz, slot)
                wires.send(("x", path, dz, way, 1, slot), piece, piece, to)

    def z_wait(path, dx, step):
        for slot in range(2):
            for way, (to, source, sign) in ZWAY.items():
                if step == 4 and slot != SLOT[way]:
                    continue
                piece = chunk(path, dx, sign * step, slot)
                wires.wait(("z", path, dx, way, step, slot), piece, source)
                if step < 3 or (step == 3 and slot == SLOT[way]):
                    wires.send(("z", path, dx, way, step + 1, slot), piece, piece, to)
        for way, (_, _, sign) in ZWAY.items():
            if step == 4 and way == "dn":
                continue
            if path == "b":
                x_send("b", 4 if step == 4 else sign * step)
            share(path, dx, 4 if step == 4 else sign * step)

    def x_wait(path, dz):
        for slot in range(2):
            for way, (to, source, sign) in XWAY.items():
                piece = chunk(path, sign, dz, slot)
                wires.wait(("x", path, dz, way, 1, slot), piece, source)
                if slot == SLOT[way]:
                    wires.send(("x", path, dz, way, 2, slot), piece, piece, to)
        for sign in (-1, 1):
            if path == "a":
                z_send("a", sign, 1)
            share(path, sign, dz)

    def x_far(path, dz):
        for way, (_, source, _) in XWAY.items():
            wires.wait(("x", path, dz, way, 2, SLOT[way]), chunk(path, 2, dz, SLOT[way]), source)
        if path == "a":
            z_send("a", 2, 1)
        share(path, 2, dz)

    x_send("a", 0)
    z_send("b", 0, 1)
    z_send("a", 0, 1)
    x_send("b", 0)
    share("a", 0, 0)
    share("b", 0, 0)
    factor_own("f1", f1, f1w, 1)

    load_f2.wait()
    for m in range(2):
        for k in range(A):
            f2t[m, :, k * W : (k + 1) * W] = f2w[m, k, lanes(y), :].T

    for kind, tag, offset, step in ORDER:
        if kind == "z":
            z_wait(tag, offset, step)
        elif kind == "x":
            (x_wait if step == 1 else x_far)(tag, offset)
        elif tag == "2":
            factor_wait("f2", f2w, True)
            for d in (1, 3, 2):
                wires.send(("d", d), dstage.at[yat(d)], dcolt.at[:, :, lanes(y)], ydev[d])
        elif step == 3:
            factor_far("f1", f1w)
            factor_own("f2", f2, f2w, 1)
        else:
            factor_wait("f1", f1w, step == 1)
            if step == 2:
                factor_own("f2", f2, f2w, 0)
    for path, dx, dz, slot in shared:
        wires.wait(("mate", path, dx, dz, slot), chunk(path, dx, dz, slot, 1), mate)
    for load in loads:
        load.wait()
    load_f1.wait()

    def tile(m, i, k):
        return store[bmap[refs[i, k, own * 2 + m]]]

    def stacked(parts):
        return jnp.concatenate(parts, axis=0)

    def give_columns(tag, turned_ref, cols_ref, m):
        for d in (1, 3, 2):
            wires.send(
                (tag, m, d), turned_ref.at[yat(d), m], cols_ref.at[m, :, :, lanes(y)], ydev[d]
            )
        own_part = local((tag, m), turned_ref.at[y, m], cols_ref.at[m, :, :, lanes(y)])
        own_part.start()
        return own_part

    def take_columns(tag, cols_ref, m, own_part):
        own_part.wait()
        for d in (1, 3, 2):
            wires.wait((tag, m, d), cols_ref.at[m, :, :, lanes(yat(-d))], ydev[4 - d])

    def spread(acc, m, first, n, out_ref, low_ref, turned_ref=None):
        for i in range(first, first + acc.shape[0] // W):
            rows = acc[(i - first) * W : (i - first + 1) * W]
            out_ref[m, i, :, n * 256 : (n + 1) * 256] = rows
            low_ref[m, i, :, n * 256 : (n + 1) * 256] = rows.astype(BF16)
            if turned_ref is not None:
                for b in range(2):
                    turned_ref[2 * n + b, m, i] = rows[:, b * W : (b + 1) * W].T.astype(BF16)

    kept1 = []
    for m in range(2):
        for n in range(2):
            acc = 0.0
            for k in range(A):
                acc += dot(
                    stacked([tile(m, i, k) for i in range(A)]), f1w[m, k, :, n * 256 : (n + 1) * 256]
                )
            spread(-acc, m, 0, n, out1, low, turned)
        kept1.append(give_columns("c1", turned, cols1, m))

    factor_wait("f2", f2w, False)
    factor_far("f2", f2w)
    for m in range(2):
        p = parent[m]
        q = [picked[m, 0], picked[m, 1]]
        for n in range(2):
            span = slice(n * 256, (n + 1) * 256)
            acc = dot(stacked([low[p, q[0]], low[p, q[1]]]), f2w[m, 0, :, span])
            for k in range(2):
                acc += dot(stacked([tile(p, q[i], q[k]) for i in range(2)]), f2w[m, k + 1, :, span])
            spread(-acc, m, 1, n, out2, low2)
            part[m, :, span] = dot(f2t[m, :, W:], stacked([low2[m, 1, :, span], low2[m, 2, :, span]]))
    keep_d.wait()
    for d in (1, 3, 2):
        wires.wait(("d", d), dcolt.at[:, :, lanes(yat(-d))], ydev[4 - d])

    def corrections(cols_ref, fw, m):
        return sum(dot(cols_ref[m, k], fw[m, k]) for k in range(A))

    def give_rows(tag, src, dst, m):
        for d in (1, 3, 2):
            wires.send((tag, m, d), src.at[yat(d), m], dst.at[m, :, lanes(y)], ydev[d])
        own_part = local((tag, m), src.at[y, m], dst.at[m, :, lanes(y)])
        own_part.start()
        return own_part

    def take_rows(tag, dst, m, own_part):
        own_part.wait()
        for d in (1, 3, 2):
            wires.wait((tag, m, d), dst.at[m, :, lanes(yat(-d))], ydev[4 - d])

    kept_diag = []
    for m in range(2):
        take_columns("c1", cols1, m, kept1[m])
        turned_diag = corrections(cols1, f1w, m)
        dlow[m] = (dcolt[m].astype(F32) - turned_diag).astype(BF16)
        for b in range(Y):
            gsend[b, m] = turned_diag[:, b * W : (b + 1) * W].T.astype(BF16)
        kept_diag.append(give_rows("g1", gsend, grow1, m))

    for m in range(2):
        p = parent[m]
        q = [picked[m, 0], picked[m, 1]]
        for n in range(2):
            span = slice(n * 256, (n + 1) * 256)
            acc = dot(dlow[p], f2w[m, 0, :, span])
            acc += dot(cols1[p, q[0]], f2w[m, 1, :, span]) + dot(cols1[p, q[1]], f2w[m, 2, :, span])
            spread(-acc, m, 0, n, out2, low2)
            term = part[m, :, span] + dot(f2t[m, :, :W], low2[m, 0, :, span])
            for b in range(Y):
                rows = term[b * W : (b + 1) * W]
                psum[m, b, :, span] = rows
                psend[m, b, :, span] = rows.astype(BF16)
        for d in (1, 3, 2):
            wires.send(("g2", m, d), psend.at[m, yat(d)], grow2.at[m, d - 1], ydev[d])
    for m in range(2):
        take_rows("g1", grow1, m, kept_diag[m])
        diag1[m] = dinv1_v[m] - grow1[m].astype(F32)
    load_dinv2.wait()
    for m in range(2):
        total = psum[m, y]
        for d in (1, 3, 2):
            wires.wait(("g2", m, d), grow2.at[m, d - 1], ydev[4 - d])
        for d in (1, 2, 3):
            total += grow2[m, d - 1].astype(F32)
        diag2[m] = dinv2_v[m] - total
    wires.finish()


def write_out(*refs):
    sources, results, sems = refs[:4], refs[4:8], refs[8]
    pairs = [(a.at[m], b.at[m]) for m in range(2) for a, b in zip(sources, results)]
    copies = [pltpu.make_async_copy(a, b, sems.at[i]) for i, (a, b) in enumerate(pairs)]
    for copy in copies:
        copy.start()
    for copy in copies:
        copy.wait()


def per_device(anc_store, block_map, anc_refs, factor1, dinv1, factor2, dinv2, parent, picked):
    any_space = pl.BlockSpec(memory_space=pl.ANY)
    vmem = pl.BlockSpec(memory_space=pltpu.VMEM)
    operands = (
        anc_store, block_map, anc_refs.transpose(1, 2, 0), factor1, dinv1, factor2, dinv2, parent, picked
    )
    flops = 2 * 2 * 2 * (9 + 3) * W * B * B
    shapes = ((2, A, W, B), (2, W, B), (2, A, W, B), (2, W, B))
    results = pl.pallas_call(
        kernel,
        out_shape=tuple(pltpu.VMEM(shape, F32) for shape in shapes),
        in_specs=[any_space] * 9,
        out_specs=(vmem,) * 4,
        scratch_shapes=[
            pltpu.SMEM((2 * X * Z * 2,), jnp.int32),
            pltpu.SMEM((2,), jnp.int32),
            pltpu.SMEM((2, 2), jnp.int32),
            pltpu.VMEM((X * Z * 4, W, B), BF16),
            pltpu.VMEM((2, A, B, B), BF16),
            pltpu.VMEM((2, A, B, B), BF16),
            pltpu.VMEM((2, B, W), F32),
            pltpu.VMEM((2, B, W), BF16),
            pltpu.SMEM((A, A, 2 * X * Z * 2), jnp.int32),
            pltpu.VMEM((2, A, W, B), BF16),
            pltpu.VMEM((2, A, W, B), BF16),
            pltpu.VMEM((Y, 2, A, W, W), BF16),
            pltpu.VMEM((2, A, W, B), BF16),
            pltpu.VMEM((2, B, B), F32),
            pltpu.VMEM((2, W, B), F32),
            pltpu.VMEM((2, W, B), F32),
            pltpu.VMEM((Y, 2, W, W), BF16),
            pltpu.VMEM((2, W, B), BF16),
            pltpu.VMEM((2, W, B), BF16),
            pltpu.VMEM((2, B, A * W), BF16),
            pltpu.VMEM((Y, 2, W, W), BF16),
            pltpu.VMEM((2, W, B), BF16),
            pltpu.VMEM((2, Y, W, B), F32),
            pltpu.VMEM((2, Y, W, B), BF16),
            pltpu.VMEM((2, 3, W, B), BF16),
            pltpu.SemaphoreType.DMA((WIRES,)),
            pltpu.SemaphoreType.DMA((WIRES,)),
            pltpu.SemaphoreType.DMA((32,)),
        ],
        compiler_params=pltpu.CompilerParams(
            collective_id=0, has_side_effects=True, vmem_limit_bytes=44 * 1024 * 1024
        ),
        cost_estimate=pl.CostEstimate(flops=flops, bytes_accessed=8 << 20, transcendentals=0),
    )(*(pltpu.with_memory_space_constraint(operand, pltpu.HBM) for operand in operands))
    return pl.pallas_call(
        write_out,
        out_shape=tuple(jax.ShapeDtypeStruct(shape, F32) for shape in shapes),
        in_specs=[vmem] * 4,
        out_specs=(any_space,) * 4,
        scratch_shapes=[pltpu.SemaphoreType.DMA((8,))],
        compiler_params=pltpu.CompilerParams(vmem_limit_bytes=4 * 1024 * 1024),
        cost_estimate=pl.CostEstimate(flops=0, bytes_accessed=8 << 20, transcendentals=0),
    )(*(pltpu.with_memory_space_constraint(result, pltpu.VMEM) for result in results))


def solution(mesh):
    return jax.shard_map(
        per_device,
        mesh=mesh,
        in_specs=(
            P("own", None, "col"),
            P(),
            P(),
            P("own", None, "col", None),
            P("own", "col", None),
            P("own", None, "col", None),
            P("own", "col", None),
            P("own"),
            P("own", None),
        ),
        out_specs=(
            P("own", None, "col", None),
            P("own", "col", None),
            P("own", None, "col", None),
            P("own", "col", None),
        ),
        check_vma=False,
    )
```
